512 devices in a mesh: dp: 32 (over z_hi, y), tensor: 16 (over x, z_lo, core).
Axes of the slice: x: 4, y: 8, z: 8 (z_hi: 4, z_lo: 2; z = z_hi * 2 + z_lo), core: 2. Of those that a mesh axis runs over, the one named last changes fastest.
Arguments:
- residual: bfloat16 [2048, 8192], P('dp', 'tensor'), may hold values from -120 to 120, as said below
- attention: bfloat16 [2048, 8192], P('dp', 'tensor'), may hold values from -18 to 18
- out_proj: bfloat16 [8192, 8192], P('tensor', 'dp'), may hold values from -0.0625 to 0.0625
- norm_gain: float32 [8192], P('tensor'), may hold values from 0.1 to 1.9
- index_draws: bfloat16 [2048, 64, 8], P('dp', 'tensor'), may hold values from -9 to 9, as said below
- labels: int32 [2048, 25], P('dp'), may hold values 0 or 1
- w_first: bfloat16 [8192, 1024], P('tensor'), may hold values from -0.0625 to 0.0625
- w_index: bfloat16 [8, 1024], replicated, may hold values from -2 to 2
- bias_first: float32 [1024], replicated, may hold values from -4 to 4
- w_hidden: bfloat16 [1024, 1024], replicated, may hold values from -0.1875 to 0.1875
- bias_hidden: float32 [1024], replicated, may hold values from -4 to 4
- w_output: bfloat16 [1024, 200], replicated, may hold values from -0.1875 to 0.1875
Outputs:
- grad_first: float32 [8192, 1024], P('tensor')
- grad_hidden: float32 [1024, 1024], P('tensor', 'dp')
- grad_output: float32 [1024, 200], P('tensor')
The draws below stay inside these ranges and needn't reach their ends.
Inputs may be any that keep to these rules, and one draw needn't show every extreme that they name: `residual`: residual entries; notes and features have unlike scales. `index_draws`: index sample entries.
All inputs are finite; a program needn't handle non-finite values. No bound on the sum of `labels` on one device may be relied on, other than what follows from the above.
Results may differ from the reference program's by a relative error of at most 0.022.
Values may be sent and summed in bfloat16 or wider, within the bound.
No kernel may reach another device: no remote copies, remote signals or barrier semaphores. Data moves between devices by JAX's collectives and lax.ppermute only.
A program may use at most 64 MiB of HBM per device.

```python
import math
import jax
import jax.numpy as jnp
from jax import lax

D = 8192
EH = 1024
CLASSES = 25
IDX = 8
SAMPLES = 64
ROWS = 64
TOKENS = 2048
N_DP = 32
N_TENSOR = 16


def draw_residual(key, part):
    key = jax.random.fold_in(key, 11)
    key_base, key_rows, key_cols = jax.random.split(key, 3)
    row_scale = jnp.exp(jax.random.uniform(key_rows, (TOKENS, 1), jnp.float32, 0.0, math.log(10.0)))
    positions = (jnp.arange(D, dtype=jnp.float32) + jax.random.uniform(key_cols, (D,), jnp.float32)) / D
    col_scale = 0.3 * jnp.exp(math.log(10.0) * positions)
    base = jnp.clip(jax.random.normal(key_base, (TOKENS, D), jnp.float32), -4.0, 4.0)
    return (base * row_scale * col_scale[None, :]).astype(jnp.bfloat16)


def draw_index_draws(key, part):
    key = jax.random.fold_in(key, 23)
    key_base, key_jitter = jax.random.split(key, 2)
    positions = (jnp.arange(SAMPLES, dtype=jnp.float32) + jax.random.uniform(key_jitter, (SAMPLES,), jnp.float32)) / SAMPLES
    sample_scale = 0.45 * jnp.exp(math.log(4.9) * positions)
    base = jnp.clip(jax.random.normal(key_base, (TOKENS, SAMPLES, IDX), jnp.float32), -4.0, 4.0)
    return (base * sample_scale[None, :, None]).astype(jnp.bfloat16)


def place_ends(entries, rng, least, high):
    shape = entries.shape
    place = [jax.random.randint(jax.random.fold_in(rng, axis), (), 0, shape[axis]) for axis in range(len(shape))]
    entries = entries.at[tuple(place)].set(least)
    longest = shape.index(max(shape))
    place[longest] = (place[longest] + 1) % shape[longest]
    return entries.at[tuple(place)].set(high)


def block_scale(stream_key, shape, cuts, least, largest):
    def one(position, blocks):
        steps = jax.random.uniform(jax.random.fold_in(jax.random.fold_in(stream_key, 6), position), (blocks,), jnp.float32, least / len(cuts), largest / len(cuts))
        return jnp.repeat(jnp.exp(steps), shape[position] // blocks).reshape((-1,) + (1,) * (len(shape) - position - 1))

    factor_of = one(*cuts[0])
    for cut in cuts[1:]:
        factor_of = factor_of * one(*cut)
    return factor_of


def centred(key, dims, scale, limit, cuts=(), held_as=jnp.bfloat16):
    factor_of = block_scale(key, dims, cuts, -0.22, 0.18) if cuts else 1.0
    values = jax.random.normal(key, dims, jnp.float32) * scale * factor_of
    return jnp.minimum(jnp.maximum(values, -limit), limit).astype(held_as)


def setup_inputs(seed: int = 0) -> dict:
    keys = jax.random.split(jax.random.key(seed), 13)
    return {
        "residual": draw_residual(jax.random.fold_in(keys[12], 71), 0),
        "attention": centred(keys[1], (TOKENS, D), 3.0, 18.0, ((0, 32), (1, 16))),
        "out_proj": centred(keys[2], (D, D), D ** -0.5, 0.0625, ((0, 16), (1, 32))),
        "norm_gain": jnp.clip(1.0 + 0.18 * jax.random.normal(keys[3], (D,), jnp.float32), 0.1, 1.9),
        "index_draws": draw_index_draws(jax.random.fold_in(keys[12], 71), 0),
        "labels": place_ends((jax.random.randint(keys[5], (TOKENS, CLASSES), 0, 4) < 1).astype(jnp.int32), jax.random.fold_in(keys[5], 1), 0, 1),
        "w_first": centred(keys[6], (D, EH), D ** -0.5, 0.0625, ((0, 16),)),
        "w_index": centred(keys[7], (IDX, EH), IDX ** -0.5, 2.0),
        "bias_first": centred(keys[8], (EH,), 1.0, 4.0, (), jnp.float32),
        "w_hidden": centred(keys[9], (EH, EH), EH ** -0.5, 0.1875),
        "bias_hidden": centred(keys[10], (EH,), 1.0, 4.0, (), jnp.float32),
        "w_output": centred(keys[11], (EH, CLASSES * IDX), EH ** -0.5, 0.1875),
    }


NORM_EPS = 1e-05

def swish(values):
    return values * jax.nn.sigmoid(values)

def swish_slope(values):
    sig = jax.nn.sigmoid(values)
    return sig * (1.0 + values * (1.0 - sig))

def rounded(values):
    return lax.optimization_barrier(values.astype(jnp.bfloat16)).astype(jnp.float32)

def contract_rows(left, right):
    return lax.dot_general(left, right, (((0,), (0,)), ((), ())), preferred_element_type=jnp.float32)

def contract_cols(left, right):
    return lax.dot_general(left, right, (((1,), (1,)), ((), ())), preferred_element_type=jnp.float32)

def reference(residual, attention, out_proj, norm_gain, index_draws, labels, w_first, w_index, bias_first, w_hidden, bias_hidden, w_output):
    block_width = D // N_TENSOR
    block_samples = SAMPLES // N_TENSOR
    pair_count = ROWS * SAMPLES
    proj_blocks = out_proj.astype(jnp.float32).reshape(N_TENSOR, block_width, D)

    def block_sum(left, right):
        left_f = left.astype(jnp.float32).reshape(ROWS, N_TENSOR, block_samples, left.shape[1])
        right_f = right.astype(jnp.float32).reshape(ROWS, N_TENSOR, block_samples, right.shape[1])
        return lax.optimization_barrier(jnp.sum(rounded(jnp.einsum('rtsa,rtsb->tab', left_f, right_f)), axis=0))

    def group(carry, number):
        start = (number * ROWS).astype(jnp.int32)
        res_rows = lax.dynamic_slice_in_dim(residual, start, ROWS, 0).astype(jnp.float32)
        att_rows = lax.dynamic_slice_in_dim(attention, start, ROWS, 0).astype(jnp.float32)
        att_rows = att_rows.reshape(ROWS, N_TENSOR, block_width)
        branch = lax.optimization_barrier(jnp.sum(rounded(jnp.einsum('rtk,tkd->rtd', att_rows, proj_blocks)), axis=1))
        state = res_rows + branch
        scale = lax.rsqrt(lax.optimization_barrier(jnp.mean(state * state, axis=1)) + NORM_EPS)
        features = (state * scale[:, None] * norm_gain).astype(jnp.bfloat16)
        first_pre = jnp.dot(features, w_first, preferred_element_type=jnp.float32)
        draws = lax.dynamic_slice_in_dim(index_draws, start, ROWS, 0).reshape(pair_count, IDX)
        index_term = jnp.dot(draws, w_index, preferred_element_type=jnp.float32).reshape(ROWS, SAMPLES, EH)
        pre_first = (first_pre[:, None, :] + index_term + bias_first).reshape(pair_count, EH)
        act_first = swish(pre_first).astype(jnp.bfloat16)
        pre_second = jnp.dot(act_first, w_hidden, preferred_element_type=jnp.float32) + bias_hidden
        act_second = swish(pre_second).astype(jnp.bfloat16)
        readout = jnp.dot(act_second, w_output, preferred_element_type=jnp.float32).reshape(pair_count, CLASSES, IDX)
        index_float = draws.astype(jnp.float32)
        logits = lax.optimization_barrier(jnp.sum(readout * index_float[:, None, :], axis=2))
        label_rows = lax.dynamic_slice_in_dim(labels, start, ROWS, 0)
        targets = jnp.broadcast_to(label_rows[:, None, :], (ROWS, SAMPLES, CLASSES)).reshape(pair_count, CLASSES).astype(jnp.float32)
        logit_grad = (jax.nn.sigmoid(logits) - targets) / SAMPLES
        out_cot = (logit_grad[:, :, None] * index_float[:, None, :]).reshape(pair_count, CLASSES * IDX).astype(jnp.bfloat16)
        output_part = block_sum(act_second, out_cot)
        second_grad = (contract_cols(out_cot, w_output) * swish_slope(pre_second)).astype(jnp.bfloat16)
        hidden_part = block_sum(act_first, second_grad)
        first_grad = (contract_cols(second_grad, w_hidden) * swish_slope(pre_first)).astype(jnp.bfloat16)
        row_grad = lax.optimization_barrier(jnp.sum(first_grad.astype(jnp.float32).reshape(ROWS, SAMPLES, EH), axis=1)).astype(jnp.bfloat16)
        first_part = rounded(contract_rows(features, row_grad))
        terms = (first_part, hidden_part, output_part)
        return (tuple((total + term for total, term in zip(carry, terms))), None)
    start_carry = (jnp.zeros((D, EH), jnp.float32), jnp.zeros((EH, EH), jnp.float32), jnp.zeros((EH, CLASSES * IDX), jnp.float32))
    totals, unused = lax.scan(group, start_carry, jnp.arange(N_DP, dtype=jnp.int32))
    first_total, hidden_total, output_total = totals
    return (first_total, hidden_total, output_total)
```

```python
import jax
import jax.numpy as jnp
from jax import lax
from jax.sharding import Mesh, PartitionSpec as P

NORM_EPS = 1e-05
bf16, f32 = jnp.bfloat16, jnp.float32
DP = ("zh", "y")
TENSOR = ("x", "zl", "c")
PARTS = {"zh": 4, "y": 8, "x": 4, "zl": 2, "c": 2}


def swish_slope(values, sig):
    return sig * (1.0 + values * (1.0 - sig))


def contract(left, right, left_dim, right_dim):
    return lax.dot_general(
        left, right, (((left_dim,), (right_dim,)), ((), ())), preferred_element_type=f32
    )


def exchange(blocks, axes):
    return lax.all_to_all(blocks, axes, 0, 0, tiled=True)


def spread(block, axes, count):
    return exchange(jnp.broadcast_to(block[None], (count,) + block.shape), axes)


def shards(
    residual,
    attention,
    out_proj,
    norm_gain,
    index_draws,
    labels,
    w_first,
    w_index,
    bias_first,
    w_hidden,
    bias_hidden,
    w_output,
):
    rows, width = residual.shape
    n_zh, n_y, n_t = PARTS["zh"], PARTS["y"], 16
    y, zl, c = lax.axis_index("y"), lax.axis_index("zl"), lax.axis_index("c")
    tensor = lax.axis_index(TENSOR)
    cols = out_proj.shape[1]
    quarter = cols // 4
    own = rows // n_t
    samples = index_draws.shape[1] * n_t
    idx = index_draws.shape[2]
    hidden = w_hidden.shape[0]
    classes = labels.shape[1]
    reads = classes * idx

    draws = exchange(index_draws.reshape(n_t, own, -1), TENSOR)
    draws = draws.reshape(n_t, own, samples // n_t, idx).transpose(1, 0, 2, 3)
    draws = draws.reshape(own * samples, idx)
    index_term = jnp.dot(draws, w_index, preferred_element_type=f32) + bias_first
    tile = (jnp.arange(reads)[None, :] % idx == jnp.arange(idx)[:, None]).astype(bf16)
    draws_rep = jnp.dot(draws, tile, preferred_element_type=f32)
    own_labels = lax.dynamic_slice_in_dim(labels, tensor * own, own, 0).astype(f32)
    targets = jnp.broadcast_to(own_labels[:, :, None], (own, classes, idx)).reshape(own, 1, reads)

    att = spread(attention, "y", n_y).reshape(n_y * rows, width)
    proj = spread(out_proj, "zh", n_zh)
    part = contract(proj, att, 1, 1).astype(bf16)
    part = part.reshape(n_zh * 2, 2, quarter, n_y * rows)
    mine = lax.dynamic_index_in_dim(part, c, 1, keepdims=False)
    other = lax.dynamic_index_in_dim(part, 1 - c, 1, keepdims=False)
    swapped = lax.ppermute(other, "c", [(0, 1), (1, 0)])
    pair = (mine.astype(f32) + swapped.astype(f32)).astype(bf16)
    branch = jnp.sum(exchange(pair, ("x", "zl")).astype(f32), axis=0).astype(bf16)
    branch = branch.reshape(quarter, n_y, rows).transpose(1, 0, 2)
    slot = (jnp.arange(4) == y // 2)[None, :, None, None]
    branch = jnp.where(slot, branch[:, None], jnp.zeros((), bf16))
    branch = exchange(branch.reshape(n_y * 4, quarter, rows), ("y", "zl", "c"))
    branch = branch.reshape(n_y, 4 * quarter, rows)
    branch = lax.dynamic_slice_in_dim(branch, 2 * (2 * zl + c), 2, 0).reshape(width, rows)

    state = residual.astype(f32).T + branch.astype(f32)
    square_sum = jnp.sum(state * state, axis=0)
    gained = (state * norm_gain[:, None]).astype(bf16)
    gained_all = lax.all_gather(gained, "zh", axis=0)
    first = contract(gained, w_first, 0, 0)
    high = square_sum.astype(bf16)
    low = (square_sum - high.astype(f32)).astype(bf16)
    extra = jnp.concatenate(
        [high[:, None], low[:, None], jnp.zeros((rows, 126), bf16)], axis=1
    )
    first = jnp.concatenate([first.astype(bf16), extra], axis=1).reshape(n_t, own, hidden + 128)
    first = jnp.sum(exchange(first, TENSOR).astype(f32), axis=0)
    square_sum = first[:, hidden] + first[:, hidden + 1]
    scale = lax.rsqrt(square_sum / (width * n_t) + NORM_EPS)
    first_pre = first[:, :hidden] * scale[:, None]

    pairs = own * samples
    pre_first = (
        first_pre[:, None, :] + index_term.reshape(own, samples, hidden)
    ).reshape(pairs, hidden)
    sig_first = jax.nn.sigmoid(pre_first)
    act_first = (pre_first * sig_first).astype(bf16)
    pre_second = jnp.dot(act_first, w_hidden, preferred_element_type=f32) + bias_hidden
    sig_second = jax.nn.sigmoid(pre_second)
    act_second = (pre_second * sig_second).astype(bf16)
    readout = jnp.dot(act_second, w_output, preferred_element_type=f32)
    same = (jnp.arange(reads)[:, None] // idx == jnp.arange(reads)[None, :] // idx).astype(f32)
    logits = jnp.dot(readout * draws_rep, same, precision=lax.Precision.HIGHEST)
    logit_grad = jax.nn.sigmoid(logits).reshape(own, samples, reads) - targets
    out_cot = (logit_grad.reshape(pairs, reads) / samples * draws_rep).astype(bf16)
    output_part = contract(act_second, out_cot, 0, 0).astype(bf16)
    second_grad = (
        contract(out_cot, w_output, 1, 1) * swish_slope(pre_second, sig_second)
    ).astype(bf16)
    hidden_part = contract(act_first, second_grad, 0, 0).astype(bf16)
    first_grad = (
        contract(second_grad, w_hidden, 1, 1) * swish_slope(pre_first, sig_first)
    ).astype(bf16)
    row_sum = jnp.sum(first_grad.reshape(own, samples, hidden), axis=1, dtype=f32)
    row_grad = (row_sum * scale[:, None]).astype(bf16)

    row_blocks = row_grad.reshape(own, n_zh, cols).transpose(1, 0, 2)
    row_blocks = jnp.broadcast_to(row_blocks[:, None], (n_zh, n_t, own, cols))
    row_blocks = exchange(row_blocks.reshape(n_zh * n_t, own, cols), ("zh",) + TENSOR)
    row_blocks = row_blocks.reshape(n_zh * rows, cols)

    pad = jnp.zeros((hidden, 256 - reads), bf16)
    weights = jnp.concatenate([hidden_part, output_part, pad], axis=1)
    weights = weights.reshape(n_t // 2, 2, hidden // n_t, hidden + 256)
    mine = lax.dynamic_index_in_dim(weights, c, 1, keepdims=False)
    other = lax.dynamic_index_in_dim(weights, 1 - c, 1, keepdims=False)
    swapped = lax.ppermute(other, "c", [(0, 1), (1, 0)])
    weights = (mine.astype(f32) + swapped.astype(f32)).astype(bf16)
    weights = jnp.sum(exchange(weights, ("x", "zl")).astype(f32), axis=0).astype(bf16)
    hidden_rows = hidden // n_t
    output_rows = weights[:, hidden:].reshape(n_y, hidden_rows // n_y, 256)
    hidden_cols = hidden // (n_zh * n_y)
    hidden_blocks = weights[:, :hidden].reshape(hidden_rows, n_zh * n_y, hidden_cols)
    hidden_blocks = hidden_blocks.transpose(1, 0, 2).reshape(n_zh * n_y, 8, 256)

    gained_all = gained_all.transpose(1, 0, 2).reshape(width, n_zh * rows)
    grads = jnp.dot(gained_all, row_blocks, preferred_element_type=f32).astype(bf16)
    grads = jnp.concatenate([grads.reshape(n_y, width // n_y, cols), output_rows], axis=1)
    grads = jnp.sum(exchange(grads, "y").astype(f32), axis=0).astype(bf16)

    grads = jnp.broadcast_to(grads[None], (n_zh * n_y,) + grads.shape)
    grads = exchange(jnp.concatenate([grads, hidden_blocks], axis=1), DP)
    grads = grads.reshape(n_zh, n_y, -1, cols)
    depth = width // n_y
    grad_first = grads[:, :, :depth].astype(f32).transpose(1, 2, 0, 3).reshape(width, hidden)
    grad_output = jnp.sum(grads[:, :, depth : depth + 8].astype(f32), axis=0)
    grad_output = grad_output.reshape(hidden_rows, 256)[:, :reads]
    grad_hidden = jnp.sum(grads[:, :, depth + 8 :].astype(f32), axis=(0, 1))
    grad_hidden = grad_hidden.reshape(hidden_rows, hidden_cols)
    return (grad_first, grad_hidden, grad_output)


def solution(mesh):
    fine = Mesh(mesh.devices.reshape(tuple(PARTS.values())), tuple(PARTS))
    placed = (
        P(DP, TENSOR),
        P(DP, TENSOR),
        P(TENSOR, DP),
        P(TENSOR),
        P(DP, TENSOR, None),
        P(DP, None),
        P(TENSOR, None),
        P(),
        P(),
        P(),
        P(),
        P(),
    )
    return jax.shard_map(
        shards,
        mesh=fine,
        in_specs=placed,
        out_specs=(P(TENSOR, None), P(TENSOR, DP), P(TENSOR, None)),
        check_vma=False,
    )
```

```python
import jax
import jax.numpy as jnp
from jax import lax
from jax.experimental import pallas as pl
from jax.experimental.pallas import tpu as pltpu
from jax.sharding import Mesh, PartitionSpec as P

NORM_EPS = 1e-05
bf16, f32 = jnp.bfloat16, jnp.float32
DP = ("zh", "y")
TENSOR = ("x", "zl", "c")
PARTS = {"zh": 4, "y": 8, "x": 4, "zl": 2, "c": 2}


def swish_slope(values, sig):
    return sig * (1.0 + values * (1.0 - sig))


def contract(left, right, left_dim, right_dim):
    return lax.dot_general(
        left, right, (((left_dim,), (right_dim,)), ((), ())), preferred_element_type=f32
    )


def exchange(blocks, axes):
    return lax.all_to_all(blocks, axes, 0, 0, tiled=True)


def spread(block, axes, count):
    return exchange(jnp.broadcast_to(block[None], (count,) + block.shape), axes)


def from_others(block, axis, count):
    return [
        lax.ppermute(block, axis, [(i, (i - k) % count) for i in range(count)])
        for k in range(1, count)
    ]


def finish_body(blocks_ref, first_ref, output_ref, hidden_ref):
    n_zh, n_y = PARTS["zh"], PARTS["y"]
    for y in range(n_y):
        for zh in range(n_zh):
            first_ref[64 * y : 64 * (y + 1), 256 * zh : 256 * (zh + 1)] = blocks_ref[
                n_y * zh + y, :64, :
            ].astype(f32)
    extra = blocks_ref[:, 64:80, :].astype(f32)
    for y in range(n_y):
        total = extra[y]
        for zh in range(1, n_zh):
            total = total + extra[n_y * zh + y]
        output_ref[8 * y : 8 * (y + 1), :] = total[:8, :200]
    hidden_ref[...] = jnp.sum(extra, axis=0)[8:]


def epinet_body(
    first_ref,
    index_ref,
    bias_first_ref,
    w_hidden_ref,
    bias_hidden_ref,
    w_output_ref,
    targets_ref,
    same_ref,
    row_ref,
    act_first_ref,
    second_grad_ref,
    act_second_ref,
    out_cot_ref,
    draws_ref,
):
    n_t, own, _ = first_ref.shape
    hidden = w_hidden_ref.shape[0]
    idx = index_ref.shape[0]
    pairs = act_first_ref.shape[0]
    lanes = pairs // (n_t * own)
    total = first_ref[0]
    for t in range(n_t):
        draws_ref[own * t : own * (t + 1), :] = first_ref[t, :, hidden:]
        if t:
            total = total + first_ref[t]
    draws = draws_ref[...]
    draws = jnp.concatenate([draws[:, idx * s : idx * (s + 1)] for s in range(lanes)], axis=0)
    spread_draws = jnp.dot(draws.astype(bf16), index_ref[...], preferred_element_type=f32)
    index_term, draws_rep = spread_draws[:, :hidden], spread_draws[:, hidden:]
    square_sum = total[:, hidden + idx * lanes : hidden + idx * lanes + 1]
    scale = lax.rsqrt(square_sum / (n_t * 512) + NORM_EPS)
    first_pre = total[:, :hidden] * scale + bias_first_ref[...]

    def per_pair(values):
        twice = jnp.concatenate([values, values], axis=0)
        twice = jnp.broadcast_to(twice[None], (pairs // (2 * own),) + twice.shape)
        return twice.reshape(pairs, values.shape[1])

    pre_first = per_pair(first_pre) + index_term
    sig_first = jax.nn.sigmoid(pre_first)
    act_first = (pre_first * sig_first).astype(bf16)
    act_first_ref[...] = act_first
    pre_second = (
        jnp.dot(act_first, w_hidden_ref[...], preferred_element_type=f32) + bias_hidden_ref[...]
    )
    sig_second = jax.nn.sigmoid(pre_second)
    act_second = (pre_second * sig_second).astype(bf16)
    act_second_ref[...] = act_second
    readout = jnp.dot(act_second, w_output_ref[...], preferred_element_type=f32)
    logits = jnp.dot(
        readout * draws_rep,
        same_ref[...],
        precision=lax.Precision.HIGHEST,
        preferred_element_type=f32,
    )
    logit_grad = (jax.nn.sigmoid(logits) - per_pair(targets_ref[...])) / (n_t * lanes)
    out_cot = (logit_grad * draws_rep).astype(bf16)
    out_cot_ref[...] = out_cot
    second_grad = (
        contract(out_cot, w_output_ref[...], 1, 1) * swish_slope(pre_second, sig_second)
    ).astype(bf16)
    second_grad_ref[...] = second_grad
    first_grad = contract(second_grad, w_hidden_ref[...], 1, 1) * swish_slope(pre_first, sig_first)
    first_grad = first_grad.astype(bf16).astype(f32)
    row_sum = jnp.sum(first_grad.reshape(pairs // (2 * own), 2 * own, hidden), axis=0)
    row_grad = (row_sum[:own] + row_sum[own:]) * scale
    row_grad = row_grad.astype(bf16)
    for t in range(n_t):
        row_ref[t] = row_grad


def weights_body(core_ref, act_first_ref, second_grad_ref, act_second_ref, out_cot_ref, mine_ref, other_ref):
    hidden = second_grad_ref.shape[1]
    blocks, rows, _ = mine_ref.shape
    low_core = core_ref[0] == 0
    for i in range(blocks):
        at = slice(2 * rows * i, 2 * rows * (i + 1))
        for left_ref, right_ref, to in (
            (act_first_ref, second_grad_ref, slice(0, hidden)),
            (act_second_ref, out_cot_ref, slice(hidden, hidden + 256)),
        ):
            both = contract(left_ref[:, at], right_ref[...], 0, 0)
            mine_ref[i, :, to] = jnp.where(low_core, both[:rows], both[rows:]).astype(bf16)
            other_ref[i, :, to] = jnp.where(low_core, both[rows:], both[:rows]).astype(bf16)


def shards(
    residual,
    attention,
    out_proj,
    norm_gain,
    index_draws,
    labels,
    w_first,
    w_index,
    bias_first,
    w_hidden,
    bias_hidden,
    w_output,
):
    rows, width = residual.shape
    n_zh, n_y, n_t = PARTS["zh"], PARTS["y"], 16
    zh = lax.axis_index("zh")
    y, zl, c = lax.axis_index("y"), lax.axis_index("zl"), lax.axis_index("c")
    tensor = lax.axis_index(TENSOR)
    cols = out_proj.shape[1]
    quarter = cols // 4
    own = rows // n_t
    samples = index_draws.shape[1] * n_t
    idx = index_draws.shape[2]
    hidden = w_hidden.shape[0]
    classes = labels.shape[1]
    reads = classes * idx

    lanes = jnp.arange(256)
    real = lanes < reads
    tile = ((lanes[None, :] % idx == jnp.arange(idx)[:, None]) & real[None, :]).astype(bf16)
    index_weights = jnp.concatenate([w_index, tile], axis=1)
    same = (lanes[:, None] // idx == lanes[None, :] // idx).astype(f32)
    w_output_wide = jnp.pad(w_output, ((0, 0), (0, 256 - reads)))
    own_labels = lax.dynamic_slice_in_dim(labels, tensor * own, own, 0).astype(f32)
    targets = jnp.broadcast_to(own_labels[:, :, None], (own, classes, idx)).reshape(own, reads)
    targets = jnp.pad(targets, ((0, 0), (0, 256 - reads)))
    att = spread(attention, "y", n_y).reshape(n_y * rows, width)
    part = jnp.zeros((n_zh, cols, n_y * rows), bf16)
    for k, proj in enumerate([out_proj] + from_others(out_proj, "zh", n_zh)):
        one = contract(proj, att, 0, 1).astype(bf16)
        part = lax.dynamic_update_index_in_dim(part, one, (zh + k) % n_zh, 0)
    part = part.reshape(n_zh * 2, 2, quarter, n_y * rows)
    mine = lax.dynamic_index_in_dim(part, c, 1, keepdims=False)
    other = lax.dynamic_index_in_dim(part, 1 - c, 1, keepdims=False)
    swapped = lax.ppermute(other, "c", [(0, 1), (1, 0)])
    pair = (mine.astype(f32) + swapped.astype(f32)).astype(bf16)
    branch = jnp.sum(exchange(pair, ("x", "zl")).astype(f32), axis=0).astype(bf16)
    branch = branch.reshape(quarter, n_y, rows).transpose(1, 0, 2)
    slot = (jnp.arange(4) == y // 2)[None, :, None, None]
    branch = jnp.where(slot, branch[:, None], jnp.zeros((), bf16))
    branch = exchange(branch.reshape(n_y * 4, quarter, rows), ("y", "zl", "c"))
    branch = branch.reshape(n_y, 4 * quarter, rows)
    branch = lax.dynamic_slice_in_dim(branch, 2 * (2 * zl + c), 2, 0).reshape(width, rows)

    state = residual.astype(f32).T + branch.astype(f32)
    square_sum = jnp.sum(state * state, axis=0)
    gained = (state * norm_gain[:, None]).astype(bf16).T
    first = jnp.dot(gained, w_first, preferred_element_type=f32)
    own_draws = samples // n_t * idx
    extra = jnp.concatenate(
        [
            index_draws.reshape(rows, own_draws).astype(f32),
            square_sum[:, None],
            jnp.zeros((rows, 127 - own_draws), f32),
        ],
        axis=1,
    )
    first = jnp.concatenate([first, extra], axis=1).reshape(n_t, own, hidden + 128)
    first = exchange(first, TENSOR)

    pairs = own * samples
    by_pair = jax.ShapeDtypeStruct((pairs, hidden), bf16)
    row_grad, act_first, second_grad, act_second, out_cot = pl.pallas_call(
        epinet_body,
        out_shape=(
            jax.ShapeDtypeStruct((n_t, own, hidden), bf16),
            by_pair,
            by_pair,
            by_pair,
            jax.ShapeDtypeStruct((pairs, 256), bf16),
        ),
        scratch_shapes=[pltpu.VMEM((rows, 128), f32)],
        compiler_params=pltpu.CompilerParams(vmem_limit_bytes=32 * 2**20),
        cost_estimate=pl.CostEstimate(
            flops=2 * 10**9, bytes_accessed=8 * 2**20, transcendentals=2**20
        ),
    )(
        first,
        index_weights,
        bias_first[None],
        w_hidden,
        bias_hidden[None],
        w_output_wide,
        targets,
        same,
    )

    row_blocks = exchange(row_grad, TENSOR).reshape(rows, n_zh, cols).transpose(1, 0, 2)
    both = jnp.broadcast_to(gained[None], (n_zh, rows, width))
    both = exchange(jnp.concatenate([both, row_blocks], axis=2), "zh").reshape(n_zh * rows, -1)
    gained_all, row_blocks = both[:, :width], both[:, width:]

    half = jax.ShapeDtypeStruct((n_t // 2, hidden // n_t, hidden + 256), bf16)
    vmem = pl.BlockSpec(memory_space=pltpu.VMEM)
    mine, other = pl.pallas_call(
        weights_body,
        out_shape=(half, half),
        in_specs=[pl.BlockSpec(memory_space=pltpu.SMEM)] + [vmem] * 4,
        compiler_params=pltpu.CompilerParams(vmem_limit_bytes=32 * 2**20),
        cost_estimate=pl.CostEstimate(
            flops=7 * 10**8, bytes_accessed=4 * 2**20, transcendentals=0
        ),
    )(c.reshape(1), act_first, second_grad, act_second, out_cot)
    swapped = lax.ppermute(other, "c", [(0, 1), (1, 0)])
    weights = (mine.astype(f32) + swapped.astype(f32)).astype(bf16)
    weights = jnp.sum(exchange(weights, ("x", "zl")).astype(f32), axis=0).astype(bf16)
    hidden_rows = hidden // n_t
    output_rows = weights[:, hidden:].reshape(n_y, hidden_rows // n_y, 256)
    hidden_cols = hidden // (n_zh * n_y)
    hidden_blocks = weights[:, :hidden].T.reshape(n_zh * n_y, 4, 8, hidden_rows)
    hidden_blocks = hidden_blocks.transpose(0, 2, 1, 3).reshape(n_zh * n_y, 8, 256)

    grads = contract(gained_all, row_blocks, 0, 0).astype(bf16)
    grads = jnp.concatenate([grads.reshape(n_y, width // n_y, cols), output_rows], axis=1)
    grads = jnp.sum(exchange(grads, "y").astype(f32), axis=0).astype(bf16)

    grads = jnp.broadcast_to(grads[None], (n_zh * n_y,) + grads.shape)
    grads = exchange(jnp.concatenate([grads, hidden_blocks], axis=1), DP)
    grad_first, grad_output, grad_hidden = pl.pallas_call(
        finish_body,
        out_shape=(
            jax.ShapeDtypeStruct((width, hidden), f32),
            jax.ShapeDtypeStruct((hidden_rows, reads), f32),
            jax.ShapeDtypeStruct((8, 256), f32),
        ),
        compiler_params=pltpu.CompilerParams(vmem_limit_bytes=24 * 2**20),
        cost_estimate=pl.CostEstimate(flops=0, bytes_accessed=4 * 2**20, transcendentals=0),
    )(grads)
    grad_hidden = grad_hidden.reshape(8, 4, hidden_rows).transpose(2, 1, 0)
    return (grad_first, grad_hidden.reshape(hidden_rows, hidden_cols), grad_output)


def solution(mesh):
    fine = Mesh(mesh.devices.reshape(tuple(PARTS.values())), tuple(PARTS))
    placed = (
        P(DP, TENSOR),
        P(DP, TENSOR),
        P(TENSOR, DP),
        P(TENSOR),
        P(DP, TENSOR, None),
        P(DP, None),
        P(TENSOR, None),
        P(),
        P(),
        P(),
        P(),
        P(),
    )
    return jax.shard_map(
        shards,
        mesh=fine,
        in_specs=placed,
        out_specs=(P(TENSOR, None), P(TENSOR, DP), P(TENSOR, None)),
        check_vma=False,
    )
```

```python
import jax
import jax.numpy as jnp
from jax import lax
from jax.experimental import pallas as pl
from jax.experimental.pallas import tpu as pltpu
from jax.sharding import Mesh, PartitionSpec as P

NORM_EPS = 1e-05
bf16, f32 = jnp.bfloat16, jnp.float32
DP = ("zh", "y")
TENSOR = ("x", "zl", "c")
PARTS = {"zh": 4, "y": 8, "x": 4, "zl": 2, "c": 2}


def swish_slope(values, sig):
    return sig * (1.0 + values * (1.0 - sig))


def contract(left, right, left_dim, right_dim):
    return lax.dot_general(
        left, right, (((left_dim,), (right_dim,)), ((), ())), preferred_element_type=f32
    )


def exchange(blocks, axes):
    return lax.all_to_all(blocks, axes, 0, 0, tiled=True)


def spread(block, axes, count):
    return exchange(jnp.broadcast_to(block[None], (count,) + block.shape), axes)


def from_further(block, axis, step):
    count = PARTS[axis]
    return lax.ppermute(block, axis, [(i, (i - step) % count) for i in range(count)])


def finish_body(blocks_ref, first_ref, output_ref, hidden_ref):
    n_zh, n_y = PARTS["zh"], PARTS["y"]
    for y in range(n_y):
        row = 256 * (y % 2) + 64 * (y // 2)
        for zh in range(n_zh):
            first_ref[row : row + 64, 256 * zh : 256 * (zh + 1)] = blocks_ref[
                n_y * zh + y, :64, :
            ].astype(f32)
    extra = blocks_ref[:, 64:80, :].astype(f32)
    for y in range(n_y):
        total = extra[y]
        for zh in range(1, n_zh):
            total = total + extra[n_y * zh + y]
        output_ref[8 * y : 8 * (y + 1), :] = total[:8, :200]
    hidden_ref[...] = jnp.sum(extra, axis=0)[8:]


def epinet_body(
    first_ref,
    index_ref,
    bias_first_ref,
    w_hidden_ref,
    bias_hidden_ref,
    w_output_ref,
    targets_ref,
    same_ref,
    row_ref,
    act_first_ref,
    second_grad_ref,
    act_second_ref,
    out_cot_ref,
    draws_ref,
):
    n_t, own, _ = first_ref.shape
    hidden = w_hidden_ref.shape[0]
    idx = index_ref.shape[0]
    pairs = act_first_ref.shape[0]
    lanes = pairs // (n_t * own)
    total = first_ref[0]
    for t in range(n_t):
        draws_ref[own * t : own * (t + 1), :] = first_ref[t, :, hidden:]
        if t:
            total = total + first_ref[t]
    draws = draws_ref[...]
    draws = jnp.concatenate([draws[:, idx * s : idx * (s + 1)] for s in range(lanes)], axis=0)
    spread_draws = jnp.dot(draws.astype(bf16), index_ref[...], preferred_element_type=f32)
    index_term, draws_rep = spread_draws[:, :hidden], spread_draws[:, hidden:]
    square_sum = total[:, hidden + idx * lanes : hidden + idx * lanes + 1]
    scale = lax.rsqrt(square_sum / (n_t * 512) + NORM_EPS)
    first_pre = total[:, :hidden] * scale + bias_first_ref[...]

    def per_pair(values):
        twice = jnp.concatenate([values, values], axis=0)
        twice = jnp.broadcast_to(twice[None], (pairs // (2 * own),) + twice.shape)
        return twice.reshape(pairs, values.shape[1])

    pre_first = per_pair(first_pre) + index_term
    sig_first = jax.nn.sigmoid(pre_first)
    act_first = (pre_first * sig_first).astype(bf16)
    act_first_ref[...] = act_first
    pre_second = (
        jnp.dot(act_first, w_hidden_ref[...], preferred_element_type=f32) + bias_hidden_ref[...]
    )
    sig_second = jax.nn.sigmoid(pre_second)
    act_second = (pre_second * sig_second).astype(bf16)
    act_second_ref[...] = act_second
    readout = jnp.dot(act_second, w_output_ref[...], preferred_element_type=f32)
    logits = jnp.dot(
        readout * draws_rep,
        same_ref[...],
        precision=lax.Precision.HIGHEST,
        preferred_element_type=f32,
    )
    logit_grad = (jax.nn.sigmoid(logits) - per_pair(targets_ref[...])) / (n_t * lanes)
    out_cot = (logit_grad * draws_rep).astype(bf16)
    out_cot_ref[...] = out_cot
    second_grad = (
        contract(out_cot, w_output_ref[...], 1, 1) * swish_slope(pre_second, sig_second)
    ).astype(bf16)
    second_grad_ref[...] = second_grad
    first_grad = contract(second_grad, w_hidden_ref[...], 1, 1) * swish_slope(pre_first, sig_first)
    first_grad = first_grad.astype(bf16).astype(f32)
    row_sum = jnp.sum(first_grad.reshape(pairs // (2 * own), 2 * own, hidden), axis=0)
    row_grad = (row_sum[:own] + row_sum[own:]) * scale
    row_grad = row_grad.astype(bf16)
    cols = row_ref.shape[2]
    for i in range(row_ref.shape[0]):
        at = i // n_t * cols
        row_ref[i] = row_grad[:, at : at + cols]


def weights_body(core_ref, act_first_ref, second_grad_ref, act_second_ref, out_cot_ref, mine_ref, other_ref):
    hidden = second_grad_ref.shape[1]
    blocks, rows, _ = mine_ref.shape
    low_core = core_ref[0] == 0
    for i in range(blocks):
        at = slice(2 * rows * i, 2 * rows * (i + 1))
        for left_ref, right_ref, to in (
            (act_first_ref, second_grad_ref, slice(0, hidden)),
            (act_second_ref, out_cot_ref, slice(hidden, hidden + 256)),
        ):
            both = contract(left_ref[:, at], right_ref[...], 0, 0)
            mine_ref[i, :, to] = jnp.where(low_core, both[:rows], both[rows:]).astype(bf16)
            other_ref[i, :, to] = jnp.where(low_core, both[rows:], both[:rows]).astype(bf16)


def shards(
    residual,
    attention,
    out_proj,
    norm_gain,
    index_draws,
    labels,
    w_first,
    w_index,
    bias_first,
    w_hidden,
    bias_hidden,
    w_output,
):
    rows, width = residual.shape
    n_zh, n_y, n_t = PARTS["zh"], PARTS["y"], 16
    zh = lax.axis_index("zh")
    y, zl, c = lax.axis_index("y"), lax.axis_index("zl"), lax.axis_index("c")
    tensor = lax.axis_index(TENSOR)
    cols = out_proj.shape[1]
    quarter = cols // 4
    own = rows // n_t
    samples = index_draws.shape[1] * n_t
    idx = index_draws.shape[2]
    hidden = w_hidden.shape[0]
    classes = labels.shape[1]
    reads = classes * idx

    lanes = jnp.arange(256)
    real = lanes < reads
    tile = ((lanes[None, :] % idx == jnp.arange(idx)[:, None]) & real[None, :]).astype(bf16)
    index_weights = jnp.concatenate([w_index, tile], axis=1)
    same = (lanes[:, None] // idx == lanes[None, :] // idx).astype(f32)
    w_output_wide = jnp.pad(w_output, ((0, 0), (0, 256 - reads)))
    own_labels = lax.dynamic_slice_in_dim(labels, tensor * own, own, 0).astype(f32)
    targets = jnp.broadcast_to(own_labels[:, :, None], (own, classes, idx)).reshape(own, reads)
    targets = jnp.pad(targets, ((0, 0), (0, 256 - reads)))
    att = spread(attention, "y", n_y).reshape(n_y * rows, width)
    half = width // 2
    ahead, behind = from_further(out_proj, "zh", 1), from_further(out_proj, "zh", -1)
    opposite = [from_further(ahead[:half], "zh", 1), from_further(behind[half:], "zh", -1)]
    part = jnp.zeros((n_zh, cols, n_y * rows), bf16)
    for k, proj in ((0, out_proj), (1, ahead), (3, behind), (2, opposite)):
        if k == 2:
            one = contract(proj[0], att[:, :half], 0, 1) + contract(proj[1], att[:, half:], 0, 1)
        else:
            one = contract(proj, att, 0, 1)
        part = lax.dynamic_update_index_in_dim(part, one.astype(bf16), (zh + k) % n_zh, 0)
    part = part.reshape(n_zh * 2, 2, quarter, n_y * rows)
    mine = lax.dynamic_index_in_dim(part, c, 1, keepdims=False)
    other = lax.dynamic_index_in_dim(part, 1 - c, 1, keepdims=False)
    swapped = lax.ppermute(other, "c", [(0, 1), (1, 0)])
    pair = (mine.astype(f32) + swapped.astype(f32)).astype(bf16)
    branch = jnp.sum(exchange(pair, ("x", "zl")).astype(f32), axis=0).astype(bf16)
    branch = exchange(branch.reshape(quarter, n_y, rows).transpose(1, 0, 2), "y")
    branch = exchange(branch.reshape(4, 2, quarter, rows), ("zl", "c")).reshape(width, rows)

    def reordered(values):
        values = values.reshape((2, 4, quarter) + values.shape[1:])
        return jnp.swapaxes(values, 0, 1).reshape((width,) + values.shape[3:])

    w_first, norm_gain = reordered(w_first), reordered(norm_gain)
    state = reordered(residual.astype(f32).T) + branch.astype(f32)
    square_sum = jnp.sum(state * state, axis=0)
    gained = (state * norm_gain[:, None]).astype(bf16).T
    first = jnp.dot(gained, w_first, preferred_element_type=f32)
    gained_all = lax.all_gather(gained, "zh", axis=0, tiled=True)
    own_draws = samples // n_t * idx
    extra = jnp.concatenate(
        [
            index_draws.reshape(rows, own_draws).astype(f32),
            square_sum[:, None],
            jnp.zeros((rows, 127 - own_draws), f32),
        ],
        axis=1,
    )
    first = jnp.concatenate([first, extra], axis=1).reshape(n_t, own, hidden + 128)
    first = exchange(first, TENSOR)

    pairs = own * samples
    by_pair = jax.ShapeDtypeStruct((pairs, hidden), bf16)
    row_blocks, act_first, second_grad, act_second, out_cot = pl.pallas_call(
        epinet_body,
        out_shape=(
            jax.ShapeDtypeStruct((n_zh * n_t, own, cols), bf16),
            by_pair,
            by_pair,
            by_pair,
            jax.ShapeDtypeStruct((pairs, 256), bf16),
        ),
        scratch_shapes=[pltpu.VMEM((rows, 128), f32)],
        compiler_params=pltpu.CompilerParams(vmem_limit_bytes=32 * 2**20),
        cost_estimate=pl.CostEstimate(
            flops=2 * 10**9, bytes_accessed=8 * 2**20, transcendentals=2**20
        ),
    )(
        first,
        index_weights,
        bias_first[None],
        w_hidden,
        bias_hidden[None],
        w_output_wide,
        targets,
        same,
    )

    row_blocks = exchange(row_blocks, ("zh",) + TENSOR).reshape(n_zh * rows, cols)

    half = jax.ShapeDtypeStruct((n_t // 2, hidden // n_t, hidden + 256), bf16)
    vmem = pl.BlockSpec(memory_space=pltpu.VMEM)
    mine, other = pl.pallas_call(
        weights_body,
        out_shape=(half, half),
        in_specs=[pl.BlockSpec(memory_space=pltpu.SMEM)] + [vmem] * 4,
        compiler_params=pltpu.CompilerParams(vmem_limit_bytes=32 * 2**20),
        cost_estimate=pl.CostEstimate(
            flops=7 * 10**8, bytes_accessed=4 * 2**20, transcendentals=0
        ),
    )(c.reshape(1), act_first, second_grad, act_second, out_cot)
    swapped = lax.ppermute(other, "c", [(0, 1), (1, 0)])
    weights = (mine.astype(f32) + swapped.astype(f32)).astype(bf16)
    weights = jnp.sum(exchange(weights, ("x", "zl")).astype(f32), axis=0).astype(bf16)
    hidden_rows = hidden // n_t
    output_rows = weights[:, hidden:].reshape(n_y, hidden_rows // n_y, 256)
    hidden_cols = hidden // (n_zh * n_y)
    hidden_blocks = weights[:, :hidden].T.reshape(n_zh * n_y, 4, 8, hidden_rows)
    hidden_blocks = hidden_blocks.transpose(0, 2, 1, 3).reshape(n_zh * n_y, 8, 256)

    grads = contract(gained_all, row_blocks, 0, 0).astype(bf16)
    grads = jnp.concatenate([grads.reshape(n_y, width // n_y, cols), output_rows], axis=1)
    grads = jnp.sum(exchange(grads, "y").astype(f32), axis=0).astype(bf16)

    grads = jnp.broadcast_to(grads[None], (n_zh * n_y,) + grads.shape)
    grads = exchange(jnp.concatenate([grads, hidden_blocks], axis=1), DP)
    grad_first, grad_output, grad_hidden = pl.pallas_call(
        finish_body,
        out_shape=(
            jax.ShapeDtypeStruct((width, hidden), f32),
            jax.ShapeDtypeStruct((hidden_rows, reads), f32),
            jax.ShapeDtypeStruct((8, 256), f32),
        ),
        compiler_params=pltpu.CompilerParams(vmem_limit_bytes=24 * 2**20),
        cost_estimate=pl.CostEstimate(flops=0, bytes_accessed=4 * 2**20, transcendentals=0),
    )(grads)
    grad_hidden = grad_hidden.reshape(8, 4, hidden_rows).transpose(2, 1, 0)
    return (grad_first, grad_hidden.reshape(hidden_rows, hidden_cols), grad_output)


def solution(mesh):
    fine = Mesh(mesh.devices.reshape(tuple(PARTS.values())), tuple(PARTS))
    placed = (
        P(DP, TENSOR),
        P(DP, TENSOR),
        P(TENSOR, DP),
        P(TENSOR),
        P(DP, TENSOR, None),
        P(DP, None),
        P(TENSOR, None),
        P(),
        P(),
        P(),
        P(),
        P(),
    )
    return jax.shard_map(
        shards,
        mesh=fine,
        in_specs=placed,
        out_specs=(P(TENSOR, None), P(TENSOR, DP), P(TENSOR, None)),
        check_vma=False,
    )
```

```python
import jax
import jax.numpy as jnp
from jax import lax
from jax.experimental import pallas as pl
from jax.experimental.pallas import tpu as pltpu
from jax.sharding import Mesh, PartitionSpec as P

NORM_EPS = 1e-05
bf16, f32 = jnp.bfloat16, jnp.float32
DP = ("zh", "y")
TENSOR = ("x", "zl", "c")
PARTS = {"zh": 4, "y": 8, "x": 4, "zl": 2, "c": 2}


def swish_slope(values, sig):
    return sig * (1.0 + values * (1.0 - sig))


def contract(left, right, left_dim, right_dim):
    return lax.dot_general(
        left, right, (((left_dim,), (right_dim,)), ((), ())), preferred_element_type=f32
    )


def exchange(blocks, axes):
    return lax.all_to_all(blocks, axes, 0, 0, tiled=True)


def spread(block, axes, count):
    return exchange(jnp.broadcast_to(block[None], (count,) + block.shape), axes)


def from_further(block, axis, step):
    count = PARTS[axis]
    return lax.ppermute(block, axis, [(i, (i - step) % count) for i in range(count)])


def finish_body(blocks_ref, first_ref, output_ref, hidden_ref):
    n_zh, n_y = PARTS["zh"], PARTS["y"]
    for y in range(n_y):
        for p in range(2):
            row = 256 * p + 64 * (y % 4) + 32 * (y // 4)
            for zh in range(n_zh):
                first_ref[row : row + 32, 256 * zh : 256 * (zh + 1)] = blocks_ref[
                    n_y * zh + y, 32 * p : 32 * (p + 1), :
                ].astype(f32)
    extra = blocks_ref[:, 64:80, :].astype(f32)
    for y in range(n_y):
        total = extra[y]
        for zh in range(1, n_zh):
            total = total + extra[n_y * zh + y]
        output_ref[8 * y : 8 * (y + 1), :] = total[:8, :200]
    hidden = jnp.sum(extra, axis=0)[8:]
    pieces = [hidden[:, :128], pltpu.roll(hidden[:, :128], 64, 1)]
    pieces += [hidden[:, 128:], pltpu.roll(hidden[:, 128:], 64, 1)]
    hidden_ref[...] = jnp.concatenate(pieces, axis=0)[:, :64]


def branch_body(parts_ref, blocks_ref):
    total = jnp.sum(parts_ref[...].astype(f32), axis=0)
    left = lax.broadcasted_iota(jnp.int32, (32, 128), 1) < 64
    for i in range(total.shape[1] // 128):
        top, bottom = total[:32, 128 * i : 128 * (i + 1)], total[32:, 128 * i : 128 * (i + 1)]
        even = jnp.where(left, top, pltpu.roll(bottom, 64, 1))
        odd = jnp.where(left, pltpu.roll(top, 64, 1), bottom)
        blocks_ref[2 * i] = even.astype(bf16)
        blocks_ref[2 * i + 1] = odd.astype(bf16)


def state_body(branch_ref, residual_ref, gain_ref, w_first_ref, extra_ref, first_ref, gained_ref):
    state = residual_ref[...].astype(f32) + branch_ref[...].astype(f32)
    square_sum = jnp.sum((state * state).T, axis=1, keepdims=True)
    square_sum = square_sum[:64] + square_sum[64:]
    gained = (state * gain_ref[...]).T
    gained = jnp.concatenate([gained[:64], gained[64:]], axis=1).astype(bf16)
    gained_ref[...] = gained
    first = jnp.dot(gained, w_first_ref[...], preferred_element_type=f32)
    extra = extra_ref[...]
    lane = lax.broadcasted_iota(jnp.int32, extra.shape, 1)
    extra = jnp.where(lane == 32, square_sum, extra)
    own, width = first_ref.shape[1], first.shape[1]
    for t in range(first_ref.shape[0]):
        first_ref[t, :, :width] = first[own * t : own * (t + 1)]
        first_ref[t, :, width:] = extra[own * t : own * (t + 1)]


def epinet_body(
    first_ref,
    index_ref,
    bias_first_ref,
    w_hidden_ref,
    bias_hidden_ref,
    w_output_ref,
    targets_ref,
    same_ref,
    row_ref,
    act_first_ref,
    second_grad_ref,
    act_second_ref,
    out_cot_ref,
    draws_ref,
):
    n_t, own, _ = first_ref.shape
    hidden = w_hidden_ref.shape[0]
    idx = index_ref.shape[0]
    pairs = act_first_ref.shape[0]
    lanes = pairs // (n_t * own)
    total = first_ref[0]
    for t in range(n_t):
        draws_ref[own * t : own * (t + 1), :] = first_ref[t, :, hidden:]
        if t:
            total = total + first_ref[t]
    draws = draws_ref[...]
    draws = jnp.concatenate([draws[:, idx * s : idx * (s + 1)] for s in range(lanes)], axis=0)
    spread_draws = jnp.dot(draws.astype(bf16), index_ref[...], preferred_element_type=f32)
    index_term, draws_rep = spread_draws[:, :hidden], spread_draws[:, hidden:]
    square_sum = total[:, hidden + idx * lanes : hidden + idx * lanes + 1]
    scale = lax.rsqrt(square_sum / (n_t * 512) + NORM_EPS)
    first_pre = total[:, :hidden] * scale + bias_first_ref[...]

    def per_pair(values):
        twice = jnp.concatenate([values, values], axis=0)
        twice = jnp.broadcast_to(twice[None], (pairs // (2 * own),) + twice.shape)
        return twice.reshape(pairs, values.shape[1])

    pre_first = per_pair(first_pre) + index_term
    sig_first = jax.nn.sigmoid(pre_first)
    act_first = (pre_first * sig_first).astype(bf16)
    act_first_ref[...] = act_first
    pre_second = (
        jnp.dot(act_first, w_hidden_ref[...], preferred_element_type=f32) + bias_hidden_ref[...]
    )
    sig_second = jax.nn.sigmoid(pre_second)
    act_second = (pre_second * sig_second).astype(bf16)
    act_second_ref[...] = act_second
    readout = jnp.dot(act_second, w_output_ref[...], preferred_element_type=f32)
    logits = jnp.dot(
        readout * draws_rep,
        same_ref[...],
        precision=lax.Precision.HIGHEST,
        preferred_element_type=f32,
    )
    logit_grad = (jax.nn.sigmoid(logits) - per_pair(targets_ref[...])) / (n_t * lanes)
    out_cot = (logit_grad * draws_rep).astype(bf16)
    out_cot_ref[...] = out_cot
    second_grad = (
        contract(out_cot, w_output_ref[...], 1, 1) * swish_slope(pre_second, sig_second)
    ).astype(bf16)
    second_grad_ref[...] = second_grad
    first_grad = contract(second_grad, w_hidden_ref[...], 1, 1) * swish_slope(pre_first, sig_first)
    first_grad = first_grad.astype(bf16).astype(f32)
    row_sum = jnp.sum(first_grad.reshape(pairs // (2 * own), 2 * own, hidden), axis=0)
    row_grad = (row_sum[:own] + row_sum[own:]) * scale
    row_grad = row_grad.astype(bf16)
    cols = row_ref.shape[2]
    for i in range(row_ref.shape[0]):
        at = i // n_t * cols
        row_ref[i] = row_grad[:, at : at + cols]


def weights_body(core_ref, act_first_ref, second_grad_ref, act_second_ref, out_cot_ref, mine_ref, other_ref):
    hidden = second_grad_ref.shape[1]
    blocks, rows, _ = mine_ref.shape
    low_core = core_ref[0] == 0
    for i in range(blocks):
        at = slice(2 * rows * i, 2 * rows * (i + 1))
        for left_ref, right_ref, to in (
            (act_first_ref, second_grad_ref, slice(0, hidden)),
            (act_second_ref, out_cot_ref, slice(hidden, hidden + 256)),
        ):
            both = contract(left_ref[:, at], right_ref[...], 0, 0)
            mine_ref[i, :, to] = jnp.where(low_core, both[:rows], both[rows:]).astype(bf16)
            other_ref[i, :, to] = jnp.where(low_core, both[rows:], both[:rows]).astype(bf16)


def shards(
    residual,
    attention,
    out_proj,
    norm_gain,
    index_draws,
    labels,
    w_first,
    w_index,
    bias_first,
    w_hidden,
    bias_hidden,
    w_output,
):
    rows, width = residual.shape
    n_zh, n_y, n_t = PARTS["zh"], PARTS["y"], 16
    zh = lax.axis_index("zh")
    y, zl, c = lax.axis_index("y"), lax.axis_index("zl"), lax.axis_index("c")
    tensor = lax.axis_index(TENSOR)
    cols = out_proj.shape[1]
    quarter = cols // 4
    own = rows // n_t
    samples = index_draws.shape[1] * n_t
    idx = index_draws.shape[2]
    hidden = w_hidden.shape[0]
    classes = labels.shape[1]
    reads = classes * idx

    lanes = jnp.arange(256)
    real = lanes < reads
    tile = ((lanes[None, :] % idx == jnp.arange(idx)[:, None]) & real[None, :]).astype(bf16)
    index_weights = jnp.concatenate([w_index, tile], axis=1)
    same = (lanes[:, None] // idx == lanes[None, :] // idx).astype(f32)
    w_output_wide = jnp.pad(w_output, ((0, 0), (0, 256 - reads)))
    own_labels = lax.dynamic_slice_in_dim(labels, tensor * own, own, 0).astype(f32)
    targets = jnp.broadcast_to(own_labels[:, :, None], (own, classes, idx)).reshape(own, reads)
    targets = jnp.pad(targets, ((0, 0), (0, 256 - reads)))
    att = spread(attention, "y", n_y).reshape(n_y * rows, width)
    half = width // 2
    ahead, behind = from_further(out_proj, "zh", 1), from_further(out_proj, "zh", -1)
    opposite = [from_further(ahead[:half], "zh", 1), from_further(behind[half:], "zh", -1)]
    part = jnp.zeros((n_zh, cols, n_y * rows), bf16)
    for k, proj in ((0, out_proj), (1, ahead), (3, behind), (2, opposite)):
        if k == 2:
            one = contract(proj[0], att[:, :half], 0, 1) + contract(proj[1], att[:, half:], 0, 1)
        else:
            one = contract(proj, att, 0, 1)
        part = lax.dynamic_update_index_in_dim(part, one.astype(bf16), (zh + k) % n_zh, 0)
    part = part.reshape(n_zh * 2, 2, quarter, n_y * rows)
    mine = lax.dynamic_index_in_dim(part, c, 1, keepdims=False)
    other = lax.dynamic_index_in_dim(part, 1 - c, 1, keepdims=False)
    swapped = lax.ppermute(other, "c", [(0, 1), (1, 0)])
    pair = (mine.astype(f32) + swapped.astype(f32)).astype(bf16)
    branch = pl.pallas_call(
        branch_body,
        out_shape=jax.ShapeDtypeStruct((n_y, 32, 128), bf16),
        compiler_params=pltpu.CompilerParams(vmem_limit_bytes=16 * 2**20),
        cost_estimate=pl.CostEstimate(flops=2**18, bytes_accessed=2**19, transcendentals=0),
    )(exchange(pair, ("x", "zl")))
    branch = exchange(exchange(branch, "y").reshape(4, 64, 128), ("zl", "c")).reshape(256, 128)

    parts = (2, 4, 2, 32)
    residual = residual.reshape((rows,) + parts).transpose(2, 1, 4, 3, 0).reshape(256, 128)
    gain = norm_gain.reshape(parts).transpose(1, 0, 3, 2)[..., None]
    gain = jnp.broadcast_to(gain, gain.shape[:-1] + (rows,)).reshape(256, 128)
    w_first = w_first.reshape(parts + (hidden,)).transpose(2, 1, 0, 3, 4).reshape(width, hidden)
    own_draws = samples // n_t * idx
    extra = index_draws.reshape(rows, own_draws).astype(f32)
    extra = jnp.pad(extra, ((0, 0), (0, 128 - own_draws)))
    first, gained = pl.pallas_call(
        state_body,
        out_shape=(
            jax.ShapeDtypeStruct((n_t, own, hidden + 128), f32),
            jax.ShapeDtypeStruct((rows, width), bf16),
        ),
        compiler_params=pltpu.CompilerParams(vmem_limit_bytes=16 * 2**20),
        cost_estimate=pl.CostEstimate(flops=2**26, bytes_accessed=2**21, transcendentals=0),
    )(branch, residual, gain, w_first, extra)
    gained_all = lax.all_gather(gained, "zh", axis=0, tiled=True)
    first = exchange(first, TENSOR)

    pairs = own * samples
    by_pair = jax.ShapeDtypeStruct((pairs, hidden), bf16)
    row_blocks, act_first, second_grad, act_second, out_cot = pl.pallas_call(
        epinet_body,
        out_shape=(
            jax.ShapeDtypeStruct((n_zh * n_t, own, cols), bf16),
            by_pair,
            by_pair,
            by_pair,
            jax.ShapeDtypeStruct((pairs, 256), bf16),
        ),
        scratch_shapes=[pltpu.VMEM((rows, 128), f32)],
        compiler_params=pltpu.CompilerParams(vmem_limit_bytes=32 * 2**20),
        cost_estimate=pl.CostEstimate(
            flops=2 * 10**9, bytes_accessed=8 * 2**20, transcendentals=2**20
        ),
    )(
        first,
        index_weights,
        bias_first[None],
        w_hidden,
        bias_hidden[None],
        w_output_wide,
        targets,
        same,
    )

    row_blocks = exchange(row_blocks, ("zh",) + TENSOR).reshape(n_zh * rows, cols)

    half = jax.ShapeDtypeStruct((n_t // 2, hidden // n_t, hidden + 256), bf16)
    vmem = pl.BlockSpec(memory_space=pltpu.VMEM)
    mine, other = pl.pallas_call(
        weights_body,
        out_shape=(half, half),
        in_specs=[pl.BlockSpec(memory_space=pltpu.SMEM)] + [vmem] * 4,
        compiler_params=pltpu.CompilerParams(vmem_limit_bytes=32 * 2**20),
        cost_estimate=pl.CostEstimate(
            flops=7 * 10**8, bytes_accessed=4 * 2**20, transcendentals=0
        ),
    )(c.reshape(1), act_first, second_grad, act_second, out_cot)
    swapped = lax.ppermute(other, "c", [(0, 1), (1, 0)])
    weights = (mine.astype(f32) + swapped.astype(f32)).astype(bf16)
    weights = jnp.sum(exchange(weights, ("x", "zl")).astype(f32), axis=0).astype(bf16)
    hidden_rows = hidden // n_t
    output_rows = weights[:, hidden:].reshape(n_y, hidden_rows // n_y, 256)
    hidden_cols = hidden // (n_zh * n_y)
    hidden_blocks = weights[:, :hidden].T.reshape(n_zh * n_y, 4, 8, hidden_rows)
    hidden_blocks = hidden_blocks.transpose(0, 2, 1, 3).reshape(n_zh * n_y, 8, 256)

    grads = contract(gained_all, row_blocks, 0, 0).astype(bf16)
    grads = jnp.concatenate([grads.reshape(n_y, width // n_y, cols), output_rows], axis=1)
    grads = jnp.sum(exchange(grads, "y").astype(f32), axis=0).astype(bf16)

    grads = jnp.broadcast_to(grads[None], (n_zh * n_y,) + grads.shape)
    grads = exchange(jnp.concatenate([grads, hidden_blocks], axis=1), DP)
    grad_first, grad_output, grad_hidden = pl.pallas_call(
        finish_body,
        out_shape=(
            jax.ShapeDtypeStruct((width, hidden), f32),
            jax.ShapeDtypeStruct((hidden_rows, reads), f32),
            jax.ShapeDtypeStruct((hidden_cols, hidden_rows), f32),
        ),
        compiler_params=pltpu.CompilerParams(vmem_limit_bytes=24 * 2**20),
        cost_estimate=pl.CostEstimate(flops=0, bytes_accessed=4 * 2**20, transcendentals=0),
    )(grads)
    return (grad_first, grad_hidden.T, grad_output)


def solution(mesh):
    fine = Mesh(mesh.devices.reshape(tuple(PARTS.values())), tuple(PARTS))
    placed = (
        P(DP, TENSOR),
        P(DP, TENSOR),
        P(TENSOR, DP),
        P(TENSOR),
        P(DP, TENSOR, None),
        P(DP, None),
        P(TENSOR, None),
        P(),
        P(),
        P(),
        P(),
        P(),
    )
    return jax.shard_map(
        shards,
        mesh=fine,
        in_specs=placed,
        out_specs=(P(TENSOR, None), P(TENSOR, DP), P(TENSOR, None)),
        check_vma=False,
    )
```

```python
import jax
import jax.numpy as jnp
from jax import lax
from jax.experimental import pallas as pl
from jax.experimental.pallas import tpu as pltpu
from jax.sharding import Mesh, PartitionSpec as P

NORM_EPS = 1e-05
bf16, f32 = jnp.bfloat16, jnp.float32
DP = ("zh", "y")
TENSOR = ("x", "zl", "c")
PARTS = {"zh": 4, "y": 8, "x": 4, "zl": 2, "c": 2}


def swish_slope(values, sig):
    return sig * (1.0 + values * (1.0 - sig))


def contract(left, right, left_dim, right_dim):
    return lax.dot_general(
        left, right, (((left_dim,), (right_dim,)), ((), ())), preferred_element_type=f32
    )


def exchange(blocks, axes):
    return lax.all_to_all(blocks, axes, 0, 0, tiled=True)


def spread(block, axes, count):
    return exchange(jnp.broadcast_to(block[None], (count,) + block.shape), axes)


def from_further(block, axis, step):
    count = PARTS[axis]
    return lax.ppermute(block, axis, [(i, (i - step) % count) for i in range(count)])


def repeat_body(block_ref, blocks_ref):
    for i in range(blocks_ref.shape[0]):
        blocks_ref[i] = block_ref[...]


def finish_body(blocks_ref, first_ref, output_ref, hidden_ref):
    n_zh, n_y = PARTS["zh"], PARTS["y"]
    for y in range(n_y):
        for p in range(2):
            row = 256 * p + 64 * (y % 4) + 32 * (y // 4)
            for zh in range(n_zh):
                first_ref[row : row + 32, 256 * zh : 256 * (zh + 1)] = blocks_ref[
                    n_y * zh + y, 32 * p : 32 * (p + 1), :
                ].astype(f32)
    extra = blocks_ref[:, 64:80, :].astype(f32)
    for y in range(n_y):
        total = extra[y]
        for zh in range(1, n_zh):
            total = total + extra[n_y * zh + y]
        output_ref[8 * y : 8 * (y + 1), :] = total[:8, :200]
    hidden = jnp.sum(extra, axis=0)[8:]
    pieces = [hidden[:, :128], pltpu.roll(hidden[:, :128], 64, 1)]
    pieces += [hidden[:, 128:], pltpu.roll(hidden[:, 128:], 64, 1)]
    hidden_ref[...] = jnp.concatenate(pieces, axis=0)[:, :64]


def branch_body(parts_ref, blocks_ref):
    total = jnp.sum(parts_ref[...].astype(f32), axis=0)
    left = lax.broadcasted_iota(jnp.int32, (32, 128), 1) < 64
    for i in range(total.shape[1] // 128):
        top, bottom = total[:32, 128 * i : 128 * (i + 1)], total[32:, 128 * i : 128 * (i + 1)]
        even = jnp.where(left, top, pltpu.roll(bottom, 64, 1))
        odd = jnp.where(left, pltpu.roll(top, 64, 1), bottom)
        blocks_ref[2 * i] = even.astype(bf16)
        blocks_ref[2 * i + 1] = odd.astype(bf16)


def state_body(branch_ref, residual_ref, gain_ref, w_first_ref, extra_ref, first_ref, gained_ref):
    state = residual_ref[...].astype(f32) + branch_ref[...].astype(f32)
    square_sum = jnp.sum((state * state).T, axis=1, keepdims=True)
    square_sum = square_sum[:64] + square_sum[64:]
    gained = (state * gain_ref[...]).T
    gained = jnp.concatenate([gained[:64], gained[64:]], axis=1).astype(bf16)
    gained_ref[...] = gained
    first = jnp.dot(gained, w_first_ref[...], preferred_element_type=f32)
    extra = extra_ref[...]
    lane = lax.broadcasted_iota(jnp.int32, extra.shape, 1)
    extra = jnp.where(lane == 32, square_sum, extra)
    own, width = first_ref.shape[1], first.shape[1]
    for t in range(first_ref.shape[0]):
        first_ref[t, :, :width] = first[own * t : own * (t + 1)]
        first_ref[t, :, width:] = extra[own * t : own * (t + 1)]


def epinet_body(
    first_ref,
    index_ref,
    bias_first_ref,
    w_hidden_ref,
    bias_hidden_ref,
    w_output_ref,
    targets_ref,
    same_ref,
    row_ref,
    act_first_ref,
    second_grad_ref,
    act_second_ref,
    out_cot_ref,
    draws_ref,
):
    n_t, own, _ = first_ref.shape
    hidden = w_hidden_ref.shape[0]
    idx = index_ref.shape[0]
    pairs = act_first_ref.shape[0]
    lanes = pairs // (n_t * own)
    total = first_ref[0]
    for t in range(n_t):
        draws_ref[own * t : own * (t + 1), :] = first_ref[t, :, hidden:]
        if t:
            total = total + first_ref[t]
    draws = draws_ref[...]
    draws = jnp.concatenate([draws[:, idx * s : idx * (s + 1)] for s in range(lanes)], axis=0)
    spread_draws = jnp.dot(draws.astype(bf16), index_ref[...], preferred_element_type=f32)
    index_term, draws_rep = spread_draws[:, :hidden], spread_draws[:, hidden:]
    square_sum = total[:, hidden + idx * lanes : hidden + idx * lanes + 1]
    scale = lax.rsqrt(square_sum / (n_t * 512) + NORM_EPS)
    first_pre = total[:, :hidden] * scale + bias_first_ref[...]

    def per_pair(values):
        twice = jnp.concatenate([values, values], axis=0)
        twice = jnp.broadcast_to(twice[None], (pairs // (2 * own),) + twice.shape)
        return twice.reshape(pairs, values.shape[1])

    pre_first = per_pair(first_pre) + index_term
    sig_first = jax.nn.sigmoid(pre_first)
    act_first = (pre_first * sig_first).astype(bf16)
    act_first_ref[...] = act_first
    pre_second = (
        jnp.dot(act_first, w_hidden_ref[...], preferred_element_type=f32) + bias_hidden_ref[...]
    )
    sig_second = jax.nn.sigmoid(pre_second)
    act_second = (pre_second * sig_second).astype(bf16)
    act_second_ref[...] = act_second
    readout = jnp.dot(act_second, w_output_ref[...], preferred_element_type=f32)
    logits = jnp.dot(
        readout * draws_rep,
        same_ref[...],
        precision=lax.Precision.HIGHEST,
        preferred_element_type=f32,
    )
    logit_grad = (jax.nn.sigmoid(logits) - per_pair(targets_ref[...])) / (n_t * lanes)
    out_cot = (logit_grad * draws_rep).astype(bf16)
    out_cot_ref[...] = out_cot
    second_grad = (
        contract(out_cot, w_output_ref[...], 1, 1) * swish_slope(pre_second, sig_second)
    ).astype(bf16)
    second_grad_ref[...] = second_grad
    first_grad = contract(second_grad, w_hidden_ref[...], 1, 1) * swish_slope(pre_first, sig_first)
    first_grad = first_grad.astype(bf16).astype(f32)
    row_sum = jnp.sum(first_grad.reshape(pairs // (2 * own), 2 * own, hidden), axis=0)
    row_grad = (row_sum[:own] + row_sum[own:]) * scale
    row_grad = row_grad.astype(bf16)
    cols = row_ref.shape[2]
    for i in range(row_ref.shape[0]):
        at = i // n_t * cols
        row_ref[i] = row_grad[:, at : at + cols]


def weights_body(core_ref, act_first_ref, second_grad_ref, act_second_ref, out_cot_ref, mine_ref, other_ref):
    hidden = second_grad_ref.shape[1]
    blocks, rows, _ = mine_ref.shape
    low_core = core_ref[0] == 0
    for i in range(blocks):
        at = slice(2 * rows * i, 2 * rows * (i + 1))
        for left_ref, right_ref, to in (
            (act_first_ref, second_grad_ref, slice(0, hidden)),
            (act_second_ref, out_cot_ref, slice(hidden, hidden + 256)),
        ):
            both = contract(left_ref[:, at], right_ref[...], 0, 0)
            mine_ref[i, :, to] = jnp.where(low_core, both[:rows], both[rows:]).astype(bf16)
            other_ref[i, :, to] = jnp.where(low_core, both[rows:], both[:rows]).astype(bf16)


def shards(
    residual,
    attention,
    out_proj,
    norm_gain,
    index_draws,
    labels,
    w_first,
    w_index,
    bias_first,
    w_hidden,
    bias_hidden,
    w_output,
):
    rows, width = residual.shape
    n_zh, n_y, n_t = PARTS["zh"], PARTS["y"], 16
    zh = lax.axis_index("zh")
    y, zl, c = lax.axis_index("y"), lax.axis_index("zl"), lax.axis_index("c")
    tensor = lax.axis_index(TENSOR)
    cols = out_proj.shape[1]
    quarter = cols // 4
    own = rows // n_t
    samples = index_draws.shape[1] * n_t
    idx = index_draws.shape[2]
    hidden = w_hidden.shape[0]
    classes = labels.shape[1]
    reads = classes * idx

    lanes = jnp.arange(256)
    real = lanes < reads
    tile = ((lanes[None, :] % idx == jnp.arange(idx)[:, None]) & real[None, :]).astype(bf16)
    index_weights = jnp.concatenate([w_index, tile], axis=1)
    same = (lanes[:, None] // idx == lanes[None, :] // idx).astype(f32)
    w_output_wide = jnp.pad(w_output, ((0, 0), (0, 256 - reads)))
    own_labels = lax.dynamic_slice_in_dim(labels, tensor * own, own, 0).astype(f32)
    targets = jnp.broadcast_to(own_labels[:, :, None], (own, classes, idx)).reshape(own, reads)
    targets = jnp.pad(targets, ((0, 0), (0, 256 - reads)))
    att = pl.pallas_call(
        repeat_body,
        out_shape=jax.ShapeDtypeStruct((n_y, rows, width), bf16),
        compiler_params=pltpu.CompilerParams(vmem_limit_bytes=16 * 2**20),
        cost_estimate=pl.CostEstimate(flops=0, bytes_accessed=9 * 2**16, transcendentals=0),
    )(attention)
    att = exchange(att, "y").reshape(n_y * rows, width)
    half = width // 2
    ahead, behind = from_further(out_proj, "zh", 1), from_further(out_proj, "zh", -1)
    opposite = [from_further(ahead[:half], "zh", 1), from_further(behind[half:], "zh", -1)]
    part = jnp.zeros((n_zh, cols, n_y * rows), bf16)
    for k, proj in ((0, out_proj), (1, ahead), (3, behind), (2, opposite)):
        if k == 2:
            one = contract(proj[0], att[:, :half], 0, 1) + contract(proj[1], att[:, half:], 0, 1)
        else:
            one = contract(proj, att, 0, 1)
        part = lax.dynamic_update_index_in_dim(part, one.astype(bf16), (zh + k) % n_zh, 0)
    part = part.reshape(n_zh * 2, 2, quarter, n_y * rows)
    mine = lax.dynamic_index_in_dim(part, c, 1, keepdims=False)
    other = lax.dynamic_index_in_dim(part, 1 - c, 1, keepdims=False)
    swapped = lax.ppermute(other, "c", [(0, 1), (1, 0)])
    pair = (mine.astype(f32) + swapped.astype(f32)).astype(bf16)
    branch = pl.pallas_call(
        branch_body,
        out_shape=jax.ShapeDtypeStruct((n_y, 32, 128), bf16),
        compiler_params=pltpu.CompilerParams(vmem_limit_bytes=16 * 2**20),
        cost_estimate=pl.CostEstimate(flops=2**18, bytes_accessed=2**19, transcendentals=0),
    )(exchange(pair, ("x", "zl")))
    branch = exchange(exchange(branch, "y").reshape(4, 64, 128), ("zl", "c")).reshape(256, 128)

    parts = (2, 4, 2, 32)
    residual = residual.reshape((rows,) + parts).transpose(2, 1, 4, 3, 0).reshape(256, 128)
    gain = norm_gain.reshape(parts).transpose(1, 0, 3, 2)[..., None]
    gain = jnp.broadcast_to(gain, gain.shape[:-1] + (rows,)).reshape(256, 128)
    w_first = w_first.reshape(parts + (hidden,)).transpose(2, 1, 0, 3, 4).reshape(width, hidden)
    own_draws = samples // n_t * idx
    extra = index_draws.reshape(rows, own_draws).astype(f32)
    extra = jnp.pad(extra, ((0, 0), (0, 128 - own_draws)))
    first, gained = pl.pallas_call(
        state_body,
        out_shape=(
            jax.ShapeDtypeStruct((n_t, own, hidden + 128), f32),
            jax.ShapeDtypeStruct((rows, width), bf16),
        ),
        compiler_params=pltpu.CompilerParams(vmem_limit_bytes=16 * 2**20),
        cost_estimate=pl.CostEstimate(flops=2**26, bytes_accessed=2**21, transcendentals=0),
    )(branch, residual, gain, w_first, extra)
    gained_all = lax.all_gather(gained, "zh", axis=0, tiled=True)
    first = exchange(first, TENSOR)

    pairs = own * samples
    by_pair = jax.ShapeDtypeStruct((pairs, hidden), bf16)
    row_blocks, act_first, second_grad, act_second, out_cot = pl.pallas_call(
        epinet_body,
        out_shape=(
            jax.ShapeDtypeStruct((n_zh * n_t, own, cols), bf16),
            by_pair,
            by_pair,
            by_pair,
            jax.ShapeDtypeStruct((pairs, 256), bf16),
        ),
        scratch_shapes=[pltpu.VMEM((rows, 128), f32)],
        compiler_params=pltpu.CompilerParams(vmem_limit_bytes=32 * 2**20),
        cost_estimate=pl.CostEstimate(
            flops=2 * 10**9, bytes_accessed=8 * 2**20, transcendentals=2**20
        ),
    )(
        first,
        index_weights,
        bias_first[None],
        w_hidden,
        bias_hidden[None],
        w_output_wide,
        targets,
        same,
    )

    row_blocks = exchange(row_blocks, ("zh",) + TENSOR).reshape(n_zh * rows, cols)

    half = jax.ShapeDtypeStruct((n_t // 2, hidden // n_t, hidden + 256), bf16)
    vmem = pl.BlockSpec(memory_space=pltpu.VMEM)
    mine, other = pl.pallas_call(
        weights_body,
        out_shape=(half, half),
        in_specs=[pl.BlockSpec(memory_space=pltpu.SMEM)] + [vmem] * 4,
        compiler_params=pltpu.CompilerParams(vmem_limit_bytes=32 * 2**20),
        cost_estimate=pl.CostEstimate(
            flops=7 * 10**8, bytes_accessed=4 * 2**20, transcendentals=0
        ),
    )(c.reshape(1), act_first, second_grad, act_second, out_cot)
    swapped = lax.ppermute(other, "c", [(0, 1), (1, 0)])
    weights = (mine.astype(f32) + swapped.astype(f32)).astype(bf16)
    weights = jnp.sum(exchange(weights, ("x", "zl")).astype(f32), axis=0).astype(bf16)
    hidden_rows = hidden // n_t
    output_rows = weights[:, hidden:].reshape(n_y, hidden_rows // n_y, 256)
    hidden_cols = hidden // (n_zh * n_y)
    hidden_blocks = weights[:, :hidden].T.reshape(n_zh * n_y, 4, 8, hidden_rows)
    hidden_blocks = hidden_blocks.transpose(0, 2, 1, 3).reshape(n_zh * n_y, 8, 256)

    grads = contract(gained_all, row_blocks, 0, 0).astype(bf16)
    grads = jnp.concatenate([grads.reshape(n_y, width // n_y, cols), output_rows], axis=1)
    grads = jnp.sum(exchange(grads, "y").astype(f32), axis=0).astype(bf16)

    grads = jnp.broadcast_to(grads[None], (n_zh * n_y,) + grads.shape)
    grads = exchange(jnp.concatenate([grads, hidden_blocks], axis=1), DP)
    grad_first, grad_output, grad_hidden = pl.pallas_call(
        finish_body,
        out_shape=(
            jax.ShapeDtypeStruct((width, hidden), f32),
            jax.ShapeDtypeStruct((hidden_rows, reads), f32),
            jax.ShapeDtypeStruct((hidden_cols, hidden_rows), f32),
        ),
        compiler_params=pltpu.CompilerParams(vmem_limit_bytes=24 * 2**20),
        cost_estimate=pl.CostEstimate(flops=0, bytes_accessed=4 * 2**20, transcendentals=0),
    )(grads)
    return (grad_first, grad_hidden.T, grad_output)


def solution(mesh):
    fine = Mesh(mesh.devices.reshape(tuple(PARTS.values())), tuple(PARTS))
    placed = (
        P(DP, TENSOR),
        P(DP, TENSOR),
        P(TENSOR, DP),
        P(TENSOR),
        P(DP, TENSOR, None),
        P(DP, None),
        P(TENSOR, None),
        P(),
        P(),
        P(),
        P(),
        P(),
    )
    return jax.shard_map(
        shards,
        mesh=fine,
        in_specs=placed,
        out_specs=(P(TENSOR, None), P(TENSOR, DP), P(TENSOR, None)),
        check_vma=False,
    )
```
